32 devices in a mesh: dp: 8 (over y, x, core), tensor: 4 (over z).
Axes of the slice: x: 2, y: 2, z: 4, core: 2. Of those that a mesh axis runs over, the one named last changes fastest.
Arguments:
- tokens: bfloat16 [2048, 8192], P('dp'), may hold values from -64 to 64
- grad_out: bfloat16 [2048, 4096], P('dp', 'tensor'), may hold values from -0.75 to 0.75
- lengths: int32 [8], P('dp'), may hold values from 128 to 256, as said below
- weights: bfloat16 [4, 8, 256, 6144], P('tensor', None, None, 'dp'), may hold values from -0.0625 to 0.0625
- moment1: float32 [4, 8, 256, 6144], P('tensor', None, None, 'dp'), may hold values from -3 to 3
- moment2: float32 [4, 8, 256, 6144], P('tensor', None, None, 'dp'), may hold values from 0.01 to 4
Outputs:
- input_grad: bfloat16 [2048, 8192], P('dp', 'tensor')
- new_weights: bfloat16 [4, 8, 256, 6144], P(None, 'dp', None, 'tensor')
- new_first: float32 [4, 8, 256, 6144], P(None, 'dp', None, 'tensor')
- new_second: float32 [4, 8, 256, 6144], P(None, 'dp', None, 'tensor')
The draws below stay inside these ranges and needn't reach their ends.
Inputs may be any that keep to these rules, and one draw needn't show every extreme that they name: `lengths`: each replica's length is at least half its slots; some replica fills all 256 slots.
All inputs are finite; a program needn't handle non-finite values.
Results may differ from the reference program's by a relative error of at most 0.04.
Values may be sent and summed in bfloat16 or wider, within the bound.
No kernel may reach another device: no remote copies, remote signals or barrier semaphores. Data moves between devices by JAX's collectives and lax.ppermute only.
A program may use at most 192 MiB of HBM per device.

```python
import math
import jax
import jax.numpy as jnp
from jax import lax

MODEL_WIDTH = 8192
QUERY_HEADS = 32
KEY_VALUE_HEADS = 8
HEAD_SIZE = 128
SEQ = 256
TOKENS = 2048
COLS = 6144
RB = 256
N_DP = 8
N_TENSOR = 4


def draw_tokens(key, part):
    key = jax.random.fold_in(key, 5)
    base = jnp.clip(jax.random.normal(key, (TOKENS, MODEL_WIDTH), jnp.float32), -6.0, 6.0)
    return base.astype(jnp.bfloat16)


def draw_lengths(key, part):
    key = jax.random.fold_in(key, 9)
    drawn = jax.random.randint(key, (N_DP,), SEQ // 2, SEQ + 1)
    filled = jax.random.randint(jax.random.fold_in(key, 1), (), 0, N_DP)
    return jnp.where(jnp.arange(N_DP) == filled, SEQ, drawn).astype(jnp.int32)


def levels(own_key, dims, shards, low, largest):
    def one(axis_at, parts):
        heights = jax.random.uniform(jax.random.fold_in(jax.random.fold_in(own_key, 6), axis_at), (parts,), jnp.float32, low / len(shards), largest / len(shards))
        return jnp.repeat(jnp.exp(heights), dims[axis_at] // parts).reshape((-1,) + (1,) * (len(dims) - axis_at - 1))

    gain = one(*shards[0])
    for cut in shards[1:]:
        gain = gain * one(*cut)
    return gain


def scatter_about(stream_key, shape, spread, bound, split=(), held_as=jnp.bfloat16):
    values = jax.random.normal(stream_key, shape, jnp.float32) * spread
    if len(split) > 0:
        values = levels(stream_key, shape, split, -0.22, 0.18) * values
    return jnp.clip(values, min=-bound, max=bound).astype(held_as)


def setup_inputs(seed: int = 0) -> dict:
    key_list = jax.random.split(jax.random.key(seed), 7)
    return {
        "tokens": draw_tokens(jax.random.fold_in(key_list[6], 71), 0),
        "grad_out": scatter_about(key_list[1], (TOKENS, QUERY_HEADS * HEAD_SIZE), 0.125, 0.75, ((0, 8), (1, 4))),
        "lengths": draw_lengths(jax.random.fold_in(key_list[6], 71), 0),
        "weights": scatter_about(key_list[3], (N_TENSOR, N_DP, RB, COLS), MODEL_WIDTH ** -0.5, 0.0625, ((0, 4), (3, 8))),
        "moment1": scatter_about(key_list[4], (N_TENSOR, N_DP, RB, COLS), 0.5, 3.0, ((0, 4), (3, 8)), jnp.float32),
        "moment2": jnp.clip(jnp.exp(math.log(4.0) - 5.9914646 * jax.random.uniform(key_list[5], (N_TENSOR, N_DP, RB, COLS), jnp.float32) ** levels(key_list[5], (N_TENSOR, N_DP, RB, COLS), ((0, 4), (3, 8)), -0.2, 0.2)), 0.01, 4.0),
    }


beta_first = 0.9
beta_second = 0.95
adam_eps = 1e-08
learn_rate = 0.002
decay_rate = 0.1
bias_first = 1.0 - beta_first ** 20
bias_second = 1.0 - beta_second ** 20

def adam_update(param, gradient, first, second):
    first_new = beta_first * first + (1.0 - beta_first) * gradient
    second_new = beta_second * second + (1.0 - beta_second) * gradient * gradient
    ratio = first_new / bias_first / (jnp.sqrt(second_new / bias_second) + adam_eps)
    widened = param.astype(jnp.float32)
    updated = (widened - learn_rate * (ratio + decay_rate * widened)).astype(jnp.bfloat16)
    return (updated, first_new, second_new)

def rounded_values(values):
    return lax.optimization_barrier(values.astype(jnp.bfloat16)).astype(jnp.float32)

def replica_grads(input_matrix, upstream_gradient, length, query_weight, key_weight, value_weight):
    sequence_length = input_matrix.shape[0]
    query_group = QUERY_HEADS // KEY_VALUE_HEADS
    scale = HEAD_SIZE ** (-0.5)
    query_rows = rounded_values(jnp.dot(input_matrix, query_weight, preferred_element_type=jnp.float32)).reshape(sequence_length, KEY_VALUE_HEADS, query_group, HEAD_SIZE)
    key_projected = rounded_values(jnp.dot(input_matrix, key_weight, preferred_element_type=jnp.float32)).reshape(sequence_length, KEY_VALUE_HEADS, HEAD_SIZE)
    value_projected = rounded_values(jnp.dot(input_matrix, value_weight, preferred_element_type=jnp.float32)).reshape(sequence_length, KEY_VALUE_HEADS, HEAD_SIZE)
    posit = jnp.arange(sequence_length)
    allowed = (posit[None, :] <= posit[:, None]) & (posit[None, :] < length)
    active_mask = (posit < length).astype(jnp.float32)
    upstream_float = upstream_gradient.astype(jnp.float32).reshape(sequence_length, KEY_VALUE_HEADS, query_group, HEAD_SIZE) * active_mask[:, None, None, None]
    scores = jnp.einsum('sgnd,tgd->gnst', query_rows, key_projected) * scale
    scores = jnp.where(allowed, scores, -jnp.inf)
    expo = jnp.exp(scores - lax.optimization_barrier(jnp.max(scores, -1, keepdims=True)))
    probs = expo / lax.optimization_barrier(jnp.sum(expo, -1, keepdims=True))
    probs_low = rounded_values(probs)
    attended = jnp.einsum('gnst,tgd->sgnd', probs_low, value_projected)
    value_gradient = jnp.einsum('xoil,ixoy->lxy', probs_low, upstream_float)
    dprobs = jnp.einsum('sgnd,tgd->gnst', upstream_float, value_projected)
    delta = jnp.transpose(lax.optimization_barrier(jnp.sum(upstream_float * attended, -1)), (1, 2, 0))[..., None]
    score_gradient = rounded_values(probs * (dprobs - delta) * scale)
    dquery = jnp.einsum('gnst,tgd->sgnd', score_gradient, key_projected).reshape(sequence_length, QUERY_HEADS * HEAD_SIZE).astype(jnp.bfloat16)
    key_gradient = jnp.einsum('xoil,ixoy->lxy', score_gradient, query_rows).reshape(sequence_length, KEY_VALUE_HEADS * HEAD_SIZE).astype(jnp.bfloat16)
    value_gradient = value_gradient.reshape(sequence_length, KEY_VALUE_HEADS * HEAD_SIZE).astype(jnp.bfloat16)
    return (dquery, key_gradient, value_gradient)

def reference(tokens, grad_out, lengths, weights, moment1, moment2):
    query_columns = QUERY_HEADS * HEAD_SIZE // N_TENSOR
    key_value_columns = KEY_VALUE_HEADS * HEAD_SIZE // N_TENSOR
    block_cols = COLS // N_TENSOR
    flat = weights.reshape(MODEL_WIDTH, COLS)
    block_list = flat.reshape(MODEL_WIDTH, N_TENSOR, block_cols)
    query_weight = block_list[:, :, :query_columns].reshape(MODEL_WIDTH, QUERY_HEADS * HEAD_SIZE)
    key_weight = block_list[:, :, query_columns:query_columns + key_value_columns].reshape(MODEL_WIDTH, KEY_VALUE_HEADS * HEAD_SIZE)
    value_weight = block_list[:, :, query_columns + key_value_columns:].reshape(MODEL_WIDTH, KEY_VALUE_HEADS * HEAD_SIZE)

    def one_replica(total, packed):
        input_matrix, upstream_gradient, length = packed
        dquery, key_gradient, value_gradient = replica_grads(input_matrix, upstream_gradient, length, query_weight, key_weight, value_weight)
        columns = jnp.concatenate([dquery.reshape(SEQ, N_TENSOR, query_columns), key_gradient.reshape(SEQ, N_TENSOR, key_value_columns), value_gradient.reshape(SEQ, N_TENSOR, key_value_columns)], 2).reshape(SEQ, COLS)
        partial_grad = rounded_values(jnp.dot(input_matrix.T, columns, preferred_element_type=jnp.float32))
        input_rows = lax.dot_general(columns, flat, (((1,), (1,)), ((), ())), preferred_element_type=jnp.float32).astype(jnp.bfloat16)
        return (total + partial_grad, input_rows)
    total, input_rows = lax.scan(one_replica, jnp.zeros((MODEL_WIDTH, COLS), jnp.float32), (tokens.reshape(N_DP, SEQ, MODEL_WIDTH), grad_out.reshape(N_DP, SEQ, QUERY_HEADS * HEAD_SIZE), lengths))
    gradient = total.reshape(weights.shape)
    new_weights, new_first, new_second = adam_update(weights, gradient, moment1, moment2)
    return (input_rows.reshape(TOKENS, MODEL_WIDTH), new_weights, new_first, new_second)
```

```python
import functools

import jax
import jax.numpy as jnp
from jax import lax
from jax.experimental import pallas as pl
from jax.experimental.pallas import tpu as pltpu
from jax.sharding import PartitionSpec as P

QUERY_HEADS = 32
KEY_VALUE_HEADS = 8
HEAD_SIZE = 128


beta_first = 0.9
beta_second = 0.95
adam_eps = 1e-08
learn_rate = 0.002
decay_rate = 0.1
bias_first = 1.0 - beta_first**20
bias_second = 1.0 - beta_second**20

MIB = 1 << 20
VMEM = pl.BlockSpec(memory_space=pltpu.VMEM)
SMEM = pl.BlockSpec(memory_space=pltpu.SMEM)


def adam_update(param, gradient, first, second):
    first_new = beta_first * first + (1.0 - beta_first) * gradient
    second_new = beta_second * second + (1.0 - beta_second) * gradient * gradient
    ratio = first_new / bias_first / (jnp.sqrt(second_new / bias_second) + adam_eps)
    widened = param.astype(jnp.float32)
    updated = (widened - learn_rate * (ratio + decay_rate * widened)).astype(jnp.bfloat16)
    return (updated, first_new, second_new)


def shape_of(dims, dtype=jnp.bfloat16):
    return jax.ShapeDtypeStruct(dims, dtype)


def size_of(arrays):
    return sum(a.size * a.dtype.itemsize for a in arrays)


def whole_call(body, outs, ins, name, flops=0, scalars=1):
    moved = size_of(ins[scalars:]) + size_of(outs)
    return pl.pallas_call(
        body,
        out_shape=outs,
        in_specs=[SMEM] * scalars + [VMEM] * (len(ins) - scalars),
        out_specs=[VMEM] * len(outs),
        compiler_params=pltpu.CompilerParams(vmem_limit_bytes=int(1.3 * moved) + 12 * MIB),
        cost_estimate=pl.CostEstimate(flops=flops, bytes_accessed=moved, transcendentals=0),
        name=name,
    )(*ins)


def after(x, *others):
    return lax.optimization_barrier((x,) + others)[0]


def pack_blocks(me, blocks):
    count = blocks.shape[0]

    def body(me_ref, in_ref, *out_refs):
        for k in range(count):
            out_refs[k][...] = in_ref[me_ref[0] ^ k].astype(jnp.bfloat16)

    return whole_call(body, [shape_of(blocks.shape[1:])] * count, [me, blocks], "pack_blocks")


def place_blocks(me, pieces):
    count = len(pieces)

    def body(me_ref, *refs):
        for k in range(count):
            refs[count][me_ref[0] ^ k] = refs[k][...]

    return whole_call(body, [shape_of((count,) + pieces[0].shape)], [me, *pieces], "place_blocks")[0]


def pack_columns(me, tokens, tensor_count, replica_count):
    length, width = tokens.shape
    rows = width // (tensor_count * replica_count)
    dims = (length, tensor_count * rows)
    if rows % 128:
        parts = tokens.reshape(length, tensor_count, replica_count, rows).transpose(2, 0, 1, 3)
        return [lax.dynamic_index_in_dim(parts, me[0] ^ k, 0, False).reshape(dims) for k in range(replica_count)]

    def body(me_ref, in_ref, *out_refs):
        for k in range(replica_count):
            for t in range(tensor_count):
                start = pl.multiple_of((t * replica_count + (me_ref[0] ^ k)) * rows, rows)
                out_refs[k][:, t * rows : (t + 1) * rows] = in_ref[:, pl.ds(start, rows)]

    return whole_call(body, [shape_of(dims)] * replica_count, [me, tokens], "pack_columns")


def place_columns(me, pieces):
    count = len(pieces)
    length, rows = pieces[0].shape
    if rows % 128:
        stacked = place_blocks(me, pieces)
        return stacked.transpose(1, 0, 2).reshape(length, count * rows)

    def body(me_ref, *refs):
        for k in range(count):
            start = pl.multiple_of((me_ref[0] ^ k) * rows, rows)
            refs[count][:, pl.ds(start, rows)] = refs[k][...]

    return whole_call(body, [shape_of((length, count * rows))], [me, *pieces], "place_columns")[0]


def swap(x, k):
    if k == 0:
        return x
    return lax.ppermute(x, "dp", [(i, i ^ k) for i in range(lax.axis_size("dp"))])


def exchange(pieces):
    return [swap(piece, k) for k, piece in enumerate(pieces)]


def over_tensor(x):
    return lax.all_to_all(x, "tensor", split_axis=0, concat_axis=0, tiled=True)


def project(pieces, weight, received=None):
    rows, depth = pieces[0].shape
    parts, columns = weight.shape[1], weight.shape[3]
    count = len(pieces)
    extra = [] if received is None else [received]
    dims = (rows, parts * columns)
    outs = [shape_of((count,) + dims)] if received is None else [shape_of(dims)] * count

    def body(*refs):
        weight_ref = refs[count]
        out_refs = refs[count + 1 + len(extra) :]
        for e in range(parts):
            block = weight_ref[:, e].reshape(depth, columns)
            cut = slice(e * columns, (e + 1) * columns)
            for k in range(count):
                value = jnp.dot(refs[k][...], block, preferred_element_type=jnp.float32)
                if received is None:
                    out_refs[0][k, :, cut] = value.astype(jnp.bfloat16)
                else:
                    value = value + refs[count + 1][k, :, cut].astype(jnp.float32)
                    out_refs[k][:, cut] = value.astype(jnp.bfloat16)

    flops = 2 * count * rows * depth * parts * columns
    return whole_call(body, outs, [*pieces, weight, *extra], "project", flops, 0)


def attention(length, terms, upstream):
    count = len(terms)
    rows, columns = terms[0].shape
    query_columns = upstream.shape[1]
    key_value_columns = (columns - query_columns) // 2
    heads = key_value_columns // HEAD_SIZE
    group = QUERY_HEADS // KEY_VALUE_HEADS
    scale = HEAD_SIZE ** (-0.5)

    def body(length_ref, *refs):
        upstream_ref, out_ref = refs[count], refs[count + 1]

        def projected(start):
            cut = slice(start, start + HEAD_SIZE)
            total = refs[0][:, cut].astype(jnp.float32)
            for term in refs[1:count]:
                total = total + term[:, cut].astype(jnp.float32)
            return total.astype(jnp.bfloat16)

        def dot(a, b, on_a, on_b):
            return lax.dot_general(a, b, (((on_a,), (on_b,)), ((), ())), preferred_element_type=jnp.float32)

        live = length_ref[0]
        at = lax.broadcasted_iota(jnp.int32, (rows, rows), 0)
        of = lax.broadcasted_iota(jnp.int32, (rows, rows), 1)
        allowed = (of <= at) & (of < live)
        active = lax.broadcasted_iota(jnp.int32, (rows, HEAD_SIZE), 0) < live
        for g in range(heads):
            key_start = query_columns + g * HEAD_SIZE
            value_start = query_columns + key_value_columns + g * HEAD_SIZE
            key, value = projected(key_start), projected(value_start)
            key_gradient = jnp.zeros((rows, HEAD_SIZE), jnp.float32)
            value_gradient = jnp.zeros((rows, HEAD_SIZE), jnp.float32)
            for n in range(group):
                start = (g * group + n) * HEAD_SIZE
                query = projected(start)
                given = upstream_ref[:, start : start + HEAD_SIZE]
                given = jnp.where(active, given, jnp.zeros_like(given))
                scores = jnp.where(allowed, dot(query, key, 1, 1) * scale, -jnp.inf)
                expo = jnp.exp(scores - jnp.max(scores, -1, keepdims=True))
                probs = expo / jnp.sum(expo, -1, keepdims=True)
                low = probs.astype(jnp.bfloat16)
                attended = dot(low, value, 1, 0)
                delta = jnp.sum(given.astype(jnp.float32) * attended, -1, keepdims=True)
                score_gradient = (probs * (dot(given, value, 1, 1) - delta) * scale).astype(jnp.bfloat16)
                out_ref[:, start : start + HEAD_SIZE] = dot(score_gradient, key, 1, 0).astype(jnp.bfloat16)
                key_gradient = key_gradient + dot(score_gradient, query, 0, 0)
                value_gradient = value_gradient + dot(low, given, 0, 0)
            out_ref[:, key_start : key_start + HEAD_SIZE] = key_gradient.astype(jnp.bfloat16)
            out_ref[:, value_start : value_start + HEAD_SIZE] = value_gradient.astype(jnp.bfloat16)

    flops = 2 * heads * group * 6 * rows * rows * HEAD_SIZE
    return whole_call(body, [shape_of((rows, columns))], [length, *terms, upstream], "attention", flops)[0]


def input_terms(columns, weight):
    tensor_count, parts, width, cut_columns = weight.shape
    count = len(columns)
    rows = columns[0].shape[0]

    def body(*refs):
        weight_ref, out_ref = refs[count], refs[count + 1]
        for k in range(count):
            total = None
            for e in range(parts):
                block = weight_ref[:, e].reshape(tensor_count * width, cut_columns)
                term = lax.dot_general(
                    refs[k][:, e * cut_columns : (e + 1) * cut_columns],
                    block,
                    (((1,), (1,)), ((), ())),
                    preferred_element_type=jnp.float32,
                )
                total = term if total is None else total + term
            for t in range(tensor_count):
                out_ref[t, k] = total[:, t * width : (t + 1) * width].astype(jnp.bfloat16)

    flops = 2 * count * rows * tensor_count * width * parts * cut_columns
    outs = [shape_of((tensor_count, count, rows, width))]
    return whole_call(body, outs, [*columns, weight], "input_terms", flops, 0)[0]


def sum_terms(terms):
    tensor_count, count, rows, width = terms.shape

    def body(in_ref, *out_refs):
        for k in range(count):
            total = in_ref[0, k].astype(jnp.float32)
            for t in range(1, tensor_count):
                total = total + in_ref[t, k].astype(jnp.float32)
            out_refs[k][...] = total.astype(jnp.bfloat16)

    return whole_call(body, [shape_of((rows, width))] * count, [terms], "sum_terms", 0, 0)


def update(pieces, columns, weight, first, second):
    tensor_count, parts, width, cut_columns = weight.shape
    count = len(pieces)
    rows = pieces[0].shape[0]
    dims = (tensor_count, 1, width, parts * cut_columns)
    if width % 128:
        inputs = jnp.concatenate(pieces, 0)
        gradient = lax.dot_general(
            inputs, jnp.concatenate(columns, 0), (((0,), (0,)), ((), ())), preferred_element_type=jnp.float32
        ).reshape(dims)
        merged = [a.transpose(0, 2, 1, 3).reshape(dims) for a in (weight, first, second)]
        return adam_update(merged[0], gradient, merged[1].astype(jnp.float32), merged[2].astype(jnp.float32))

    def body(*refs):
        weight_ref, first_ref, second_ref, new_weight, new_first, new_second = refs[2 * count :]
        gradient = None
        for k in range(count):
            term = lax.dot_general(
                refs[k][...], refs[count + k][...], (((0,), (0,)), ((), ())), preferred_element_type=jnp.float32
            )
            gradient = term if gradient is None else gradient + term
        updated, moved_first, moved_second = adam_update(
            weight_ref[0, 0],
            gradient,
            first_ref[0, 0].astype(jnp.float32),
            second_ref[0, 0].astype(jnp.float32),
        )
        new_weight[0, 0] = updated
        new_first[0, 0] = moved_first
        new_second[0, 0] = moved_second

    old = pl.BlockSpec((1, 1, width, cut_columns), lambda e, t: (t, e, 0, 0))
    new = pl.BlockSpec((1, 1, width, cut_columns), lambda e, t: (t, 0, 0, e))
    outs = [shape_of(dims), shape_of(dims, jnp.float32), shape_of(dims, jnp.float32)]
    ins = [*pieces, *columns, weight, first, second]
    return pl.pallas_call(
        body,
        grid=(parts, tensor_count),
        out_shape=outs,
        in_specs=[pl.BlockSpec((rows, width), lambda e, t: (0, t))] * count
        + [pl.BlockSpec((rows, cut_columns), lambda e, t: (0, e))] * count
        + [old] * 3,
        out_specs=[new] * 3,
        compiler_params=pltpu.CompilerParams(vmem_limit_bytes=40 * MIB),
        cost_estimate=pl.CostEstimate(
            flops=2 * count * rows * tensor_count * width * parts * cut_columns,
            bytes_accessed=size_of(ins) + size_of(outs),
            transcendentals=0,
        ),
        name="update",
    )(*ins)


def local(tokens, grad_out, lengths, weights, moment1, moment2):
    tensor_count = lax.axis_size("tensor")
    replica_count = lax.axis_size("dp")
    width, cut_columns = weights.shape[2:]
    parts = replica_count // tensor_count
    me = lax.axis_index("dp").astype(jnp.int32).reshape(1)
    new_split = (tensor_count, parts, width, cut_columns)

    weight_pieces = exchange(pack_blocks(me, weights[0]))
    weight_rows = place_blocks(me, weight_pieces)
    weight = over_tensor(weight_rows).reshape(new_split)

    token_pieces = exchange(pack_columns(me, tokens, tensor_count, replica_count))

    first_rows = place_blocks(me, exchange(pack_blocks(me, after(moment1[0], weight_rows))))
    first = over_tensor(first_rows).reshape(new_split)
    second_rows = place_blocks(me, exchange(pack_blocks(me, after(moment2[0], weight))))
    second = over_tensor(second_rows).reshape(new_split)

    sent = project(token_pieces[1::2], weight)[0]
    sums = project(token_pieces[0::2], weight, swap(sent, 1))
    terms = [swap(term, 2 * m) for m, term in enumerate(sums)]
    columns = attention(lengths, terms, grad_out)

    same_core = [swap(columns, 2 * m) for m in range(replica_count // 2)]
    other_core = [swap(x, 1) for x in same_core]
    all_columns = [x for pair in zip(same_core, other_core) for x in pair]

    moved = over_tensor(input_terms(all_columns, weight))
    input_grad = place_columns(me, exchange(sum_terms(moved)))
    new_weights, new_first, new_second = update(token_pieces, all_columns, weight, first, second)
    return (input_grad, new_weights, new_first, new_second)


def solution(mesh):
    return jax.shard_map(
        local,
        mesh=mesh,
        in_specs=(
            P("dp", None),
            P("dp", "tensor"),
            P("dp"),
            P("tensor", None, None, "dp"),
            P("tensor", None, None, "dp"),
            P("tensor", None, None, "dp"),
        ),
        out_specs=(
            P("dp", "tensor"),
            P(None, "dp", None, "tensor"),
            P(None, "dp", None, "tensor"),
            P(None, "dp", None, "tensor"),
        ),
        check_vma=False,
    )
```

```python
import functools

import jax
import jax.numpy as jnp
from jax import lax
from jax.experimental import pallas as pl
from jax.experimental.pallas import tpu as pltpu
from jax.sharding import PartitionSpec as P

QUERY_HEADS = 32
KEY_VALUE_HEADS = 8
HEAD_SIZE = 128


beta_first = 0.9
beta_second = 0.95
adam_eps = 1e-08
learn_rate = 0.002
decay_rate = 0.1
bias_first = 1.0 - beta_first**20
bias_second = 1.0 - beta_second**20

MIB = 1 << 20
MICROSECOND = 10**9
SMEM = pl.BlockSpec(memory_space=pltpu.SMEM)


def adam_update(param, gradient, first, second):
    first_new = beta_first * first + (1.0 - beta_first) * gradient
    second_new = beta_second * second + (1.0 - beta_second) * gradient * gradient
    ratio = first_new / bias_first / (jnp.sqrt(second_new / bias_second) + adam_eps)
    widened = param.astype(jnp.float32)
    updated = (widened - learn_rate * (ratio + decay_rate * widened)).astype(jnp.bfloat16)
    return (updated, first_new, second_new)


def shape_of(dims, dtype=jnp.bfloat16):
    return jax.ShapeDtypeStruct(dims, dtype)


def size_of(arrays):
    return sum(a.size * a.dtype.itemsize for a in arrays)


def whole_block(operand):
    if isinstance(operand, tuple):
        dims, at = operand[0].shape[1:], operand[1]
        return pl.BlockSpec((None,) + tuple(dims), lambda i: (at,) + (0,) * len(dims))
    dims = operand.shape
    return pl.BlockSpec(tuple(dims), lambda i: (0,) * len(dims))


def array_of(operand):
    return operand[0] if isinstance(operand, tuple) else operand


def whole_call(body, outs, ins, name, flops=0, scalars=1, waits=()):
    arrays = [array_of(x) for x in ins]
    moved = size_of(arrays[scalars:]) + size_of(outs)
    count = len(ins)

    def without(*refs):
        body(*refs[:count], *refs[count + len(waits) :])

    call = pl.pallas_call(
        without,
        grid=(1,),
        out_shape=outs,
        in_specs=[SMEM] * scalars
        + [whole_block(x) for x in ins[scalars:]]
        + [pl.BlockSpec(memory_space=pl.ANY)] * len(waits),
        out_specs=[whole_block(x) for x in outs],
        compiler_params=pltpu.CompilerParams(vmem_limit_bytes=60 * MIB),
        cost_estimate=pl.CostEstimate(flops=0, bytes_accessed=0, transcendentals=0),
        name=name,
    )
    return list(call(*arrays, *waits))


def pack_blocks(me, blocks, first=0, last=None):
    count, rows, columns = blocks.shape
    last = rows if last is None else last

    def body(me_ref, in_ref, *out_refs):
        for k in range(count):
            out_refs[k // 2][k % 2] = in_ref[me_ref[0] ^ k, first:last].astype(jnp.bfloat16)

    return whole_call(body, [shape_of((2, last - first, columns))] * (count // 2), [me, blocks], "pack_blocks")


def merge_rows(low, high):
    tensor_count, parts, rows, columns = low.shape

    def body(low_ref, high_ref, out_ref):
        out_ref[:, :, :rows] = low_ref[...]
        out_ref[:, :, rows:] = high_ref[...]

    outs = [shape_of((tensor_count, parts, rows + high.shape[2], columns))]
    return whole_call(body, outs, [low, high], "merge_rows", scalars=0)[0]


def gate(pieces, waits, cost=0):
    count = len(pieces)
    anywhere = pl.BlockSpec(memory_space=pl.ANY)
    return list(pl.pallas_call(
        lambda *refs: None,
        out_shape=[shape_of(x.shape, x.dtype) for x in pieces],
        in_specs=[anywhere] * (count + len(waits)),
        out_specs=[anywhere] * count,
        input_output_aliases={i: i for i in range(count)},
        cost_estimate=pl.CostEstimate(flops=cost * MICROSECOND, bytes_accessed=0, transcendentals=0),
        name="gate",
    )(*pieces, *waits))


def place_blocks(me, pieces, waits=()):
    count = len(pieces)
    dims = array_of(pieces[0]).shape[-2:]

    def body(me_ref, *refs):
        for k in range(count):
            refs[count][me_ref[0] ^ k] = refs[k][...]

    return whole_call(body, [shape_of((count,) + dims)], [me, *pieces], "place_blocks", waits=waits)[0]


def pack_columns(me, tokens, tensor_count, replica_count, waits=()):
    length, width = tokens.shape
    rows = width // (tensor_count * replica_count)
    chips = replica_count // 2
    dims = (2, length, tensor_count * rows)
    if rows % 128:
        parts = tokens.reshape(length, tensor_count, replica_count, rows).transpose(2, 0, 1, 3)
        pieces = [lax.dynamic_index_in_dim(parts, me[0] ^ k, 0, False) for k in range(replica_count)]
        return [jnp.stack(pieces[2 * m : 2 * m + 2]).reshape(dims) for m in range(chips)]

    def body(me_ref, in_ref, *out_refs):
        for k in range(replica_count):
            for t in range(tensor_count):
                start = pl.multiple_of((t * replica_count + (me_ref[0] ^ k)) * rows, rows)
                out_refs[k // 2][k % 2, :, t * rows : (t + 1) * rows] = in_ref[:, pl.ds(start, rows)]

    return whole_call(body, [shape_of(dims)] * chips, [me, tokens], "pack_columns", waits=waits)


def place_columns(me, pieces, waits=()):
    count = len(pieces)
    length, rows = array_of(pieces[0]).shape[-2:]
    if rows % 128:
        stacked = place_blocks(me, pieces)
        return stacked.transpose(1, 0, 2).reshape(length, count * rows)

    def body(me_ref, *refs):
        for k in range(count):
            start = pl.multiple_of((me_ref[0] ^ k) * rows, rows)
            refs[count][:, pl.ds(start, rows)] = refs[k][...]

    return whole_call(body, [shape_of((length, count * rows))], [me, *pieces], "place_columns", waits=waits)[0]


def swap(x, k):
    if k == 0:
        return x
    return lax.ppermute(x, "dp", [(i, i ^ k) for i in range(lax.axis_size("dp"))])


def swap_tensor(x, j):
    return lax.ppermute(x, "tensor", [(i, i ^ j) for i in range(lax.axis_size("tensor"))])


def to_chips(pairs):
    return [swap(x, 2 * m) for m, x in enumerate(pairs)]


def to_cores(pairs):
    return [view for x in pairs for view in ((x, 0), (swap(x, 1), 1))]


def exchange(pieces):
    return [swap(piece, k) for k, piece in enumerate(pieces)]


def over_tensor(x):
    return lax.all_to_all(x, "tensor", split_axis=0, concat_axis=0, tiled=True)


def project(pairs, weights):
    _, rows, depth = pairs[0].shape
    parts, columns = weights[0].shape[1], weights[0].shape[3]
    count = len(pairs)

    def body(*refs):
        for e in range(parts):
            blocks = [refs[count + at][:, e].reshape(depth, columns) for at in range(2)]
            for k in range(count):
                value = jnp.dot(refs[k][0], blocks[0], preferred_element_type=jnp.float32)
                value = value + jnp.dot(refs[k][1], blocks[1], preferred_element_type=jnp.float32)
                refs[count + 2 + k][:, e * columns : (e + 1) * columns] = value.astype(jnp.bfloat16)

    return whole_call(body, [shape_of((rows, parts * columns))] * count, [*pairs, *weights], "project", scalars=0)


def attention(length, terms, upstream, waits=()):
    count = len(terms)
    rows, columns = terms[0].shape
    query_columns = upstream.shape[1]
    key_value_columns = (columns - query_columns) // 2
    heads = key_value_columns // HEAD_SIZE
    group = QUERY_HEADS // KEY_VALUE_HEADS
    scale = HEAD_SIZE ** (-0.5)

    def body(length_ref, *refs):
        upstream_ref, out_refs = refs[count], refs[count + 1 :]

        def projected(start):
            cut = slice(start, start + HEAD_SIZE)
            total = refs[0][:, cut].astype(jnp.float32)
            for term in refs[1:count]:
                total = total + term[:, cut].astype(jnp.float32)
            return total.astype(jnp.bfloat16)

        def dot(a, b, on_a, on_b):
            return lax.dot_general(a, b, (((on_a,), (on_b,)), ((), ())), preferred_element_type=jnp.float32)

        def store(start, value):
            for out_ref in out_refs:
                out_ref[:, start : start + HEAD_SIZE] = value.astype(jnp.bfloat16)

        live = length_ref[0]
        at = lax.broadcasted_iota(jnp.int32, (rows, rows), 0)
        of = lax.broadcasted_iota(jnp.int32, (rows, rows), 1)
        allowed = (of <= at) & (of < live)
        active = lax.broadcasted_iota(jnp.int32, (rows, HEAD_SIZE), 0) < live
        for g in range(heads):
            key_start = query_columns + g * HEAD_SIZE
            value_start = query_columns + key_value_columns + g * HEAD_SIZE
            key, value = projected(key_start), projected(value_start)
            key_gradient = jnp.zeros((rows, HEAD_SIZE), jnp.float32)
            value_gradient = jnp.zeros((rows, HEAD_SIZE), jnp.float32)
            for n in range(group):
                start = (g * group + n) * HEAD_SIZE
                query = projected(start)
                given = upstream_ref[:, start : start + HEAD_SIZE]
                given = jnp.where(active, given, jnp.zeros_like(given))
                scores = jnp.where(allowed, dot(query, key, 1, 1) * scale, -jnp.inf)
                expo = jnp.exp(scores - jnp.max(scores, -1, keepdims=True))
                probs = expo / jnp.sum(expo, -1, keepdims=True)
                low = probs.astype(jnp.bfloat16)
                attended = dot(low, value, 1, 0)
                delta = jnp.sum(given.astype(jnp.float32) * attended, -1, keepdims=True)
                score_gradient = (probs * (dot(given, value, 1, 1) - delta) * scale).astype(jnp.bfloat16)
                store(start, dot(score_gradient, key, 1, 0))
                key_gradient = key_gradient + dot(score_gradient, query, 0, 0)
                value_gradient = value_gradient + dot(low, given, 0, 0)
            store(key_start, key_gradient)
            store(value_start, value_gradient)

    flops = 2 * heads * group * 6 * rows * rows * HEAD_SIZE
    return whole_call(body, [shape_of((rows, columns))] * 2, [length, *terms, upstream], "attention", flops, waits=waits)


def halving_order(count):
    if count == 1:
        return [0]
    half = [2 * j for j in halving_order(count // 2)]
    return half + [j + 1 for j in half]


def input_terms(place, columns, weights):
    tensor_count, parts, width, cut_columns = weights[0].shape
    count = len(columns)
    rows = columns[0].shape[0]
    half = tensor_count // 2
    order = halving_order(tensor_count)

    def body(place_ref, *refs):
        for at, j in enumerate(order):
            for core in range(2):
                blocks = [refs[count + core][place_ref[0] ^ j, e] for e in range(parts)]
                for k in range(count):
                    total = None
                    for e in range(parts):
                        term = lax.dot_general(
                            refs[k][:, e * cut_columns : (e + 1) * cut_columns],
                            blocks[e],
                            (((1,), (1,)), ((), ())),
                            preferred_element_type=jnp.float32,
                        )
                        total = term if total is None else total + term
                    refs[count + 2 + at // half][at % half, 2 * k + core] = total.astype(jnp.bfloat16)

    outs = [shape_of((half, 2 * count, rows, width))] * 2
    return whole_call(body, outs, [place, *columns, *weights], "input_terms")


def fold_terms(kept, received):
    half = kept.shape[0] // 2
    dims = (half,) + kept.shape[1:]

    def body(kept_ref, received_ref, stay_ref, go_ref):
        for at in range(2 * half):
            total = kept_ref[at].astype(jnp.float32) + received_ref[at].astype(jnp.float32)
            if at < half:
                stay_ref[at] = total
            else:
                go_ref[at - half] = total.astype(jnp.bfloat16)

    outs = [shape_of(dims, jnp.float32), shape_of(dims)]
    return whole_call(body, outs, [kept, received], "fold_terms", scalars=0)


def sum_terms(kept, received, waits=()):
    count = kept.shape[1] // 2

    def body(kept_ref, received_ref, *out_refs):
        for k in range(2 * count):
            total = kept_ref[0, k].astype(jnp.float32) + received_ref[0, k].astype(jnp.float32)
            out_refs[k // 2][k % 2] = total.astype(jnp.bfloat16)

    outs = [shape_of((2,) + kept.shape[2:])] * count
    return whole_call(body, outs, [kept, received], "sum_terms", scalars=0, waits=waits)


def update(pieces, columns, weight, first, second, begin, end, earlier=(), waits=()):
    tensor_count, parts, width, cut_columns = weight.shape
    count = len(pieces)
    rows = columns[0].shape[0]
    dims = (tensor_count, 1, width, parts * cut_columns)
    if width % 128:
        if earlier:
            return earlier
        inputs = jnp.concatenate([x[at] for x, at in pieces], 0)
        gradient = lax.dot_general(
            inputs, jnp.concatenate(columns, 0), (((0,), (0,)), ((), ())), preferred_element_type=jnp.float32
        ).reshape(dims)
        merged = [a.transpose(0, 2, 1, 3).reshape(dims) for a in (weight, first, second)]
        return adam_update(merged[0], gradient, merged[1].astype(jnp.float32), merged[2].astype(jnp.float32))

    def body(*refs):
        weight_ref, first_ref, second_ref = refs[2 * count : 2 * count + 3]
        new_weight, new_first, new_second = refs[-3:]
        gradient = None
        cut = pl.ds(pl.multiple_of(pl.program_id(1) * cut_columns, cut_columns), cut_columns)
        for k in range(count):
            term = lax.dot_general(
                refs[k][...], refs[count + k][:, cut], (((0,), (0,)), ((), ())), preferred_element_type=jnp.float32
            )
            gradient = term if gradient is None else gradient + term
        updated, moved_first, moved_second = adam_update(
            weight_ref[0, 0],
            gradient,
            first_ref[0, 0].astype(jnp.float32),
            second_ref[0, 0].astype(jnp.float32),
        )
        new_weight[0, 0] = updated
        new_first[0, 0] = moved_first
        new_second[0, 0] = moved_second

    old = pl.BlockSpec((1, 1, width, cut_columns), lambda t, e: (begin + t, e, 0, 0))
    new = pl.BlockSpec((1, 1, width, cut_columns), lambda t, e: (begin + t, 0, 0, e))
    outs = [shape_of(dims), shape_of(dims, jnp.float32), shape_of(dims, jnp.float32)]
    ins = [*map(array_of, pieces), *columns, weight, first, second, *earlier, *waits]
    given = len(ins) - len(earlier) - len(waits)
    call = pl.pallas_call(
        body,
        grid=(end - begin, parts),
        out_shape=outs,
        in_specs=[pl.BlockSpec((None, rows, width), lambda t, e, at=at: (at, 0, begin + t)) for _, at in pieces]
        + [pl.BlockSpec((rows, parts * cut_columns), lambda t, e: (0, 0))] * count
        + [old] * 3
        + [pl.BlockSpec(memory_space=pl.ANY)] * (len(earlier) + len(waits)),
        out_specs=[new] * 3,
        input_output_aliases={given + i: i for i in range(len(earlier))},
        compiler_params=pltpu.CompilerParams(vmem_limit_bytes=60 * MIB),
        cost_estimate=pl.CostEstimate(flops=0, bytes_accessed=0, transcendentals=0),
        name="update",
    )
    return list(call(*ins))


def local(tokens, grad_out, lengths, weights, moment1, moment2):
    tensor_count = lax.axis_size("tensor")
    replica_count = lax.axis_size("dp")
    width, cut_columns = weights.shape[2:]
    parts = replica_count // tensor_count
    me = lax.axis_index("dp").astype(jnp.int32).reshape(1)
    place = lax.axis_index("tensor").astype(jnp.int32).reshape(1)
    new_split = (tensor_count, parts, width, cut_columns)

    chips = replica_count // 2

    def next_transfer(received, following, meanwhile=(), cost=0):
        held = gate(received[1:] + following, meanwhile, cost)
        return received[:1] + held[: chips - 1], held[chips - 1 :]

    cut = max(width * 6 // 16 // 16, 1) * 16
    packed_low, packed_high = pack_blocks(me, weights[0], 0, cut), pack_blocks(me, weights[0], cut)
    packed_first = pack_blocks(me, moment1[0])
    packed_second = pack_blocks(me, moment2[0])
    received, packed_high = next_transfer(to_chips(packed_low), packed_high, packed_first[:1], 8)
    low_rows = place_blocks(me, to_cores(received))
    packed_tokens = pack_columns(me, tokens, tensor_count, replica_count, (low_rows,))
    received, packed_first = next_transfer(
        to_chips(packed_high), packed_first, [packed_tokens[0]], 15
    )
    high_rows = place_blocks(me, to_cores(received))
    weight = merge_rows(
        *(over_tensor(x).reshape(tensor_count, parts, x.shape[1], cut_columns) for x in (low_rows, high_rows))
    )
    received, packed_tokens = next_transfer(to_chips(packed_first), packed_tokens, [high_rows, packed_second[0]], 15)
    first_rows = place_blocks(me, to_cores(received))
    first = over_tensor(first_rows).reshape(new_split)
    token_pairs, packed_second = next_transfer(
        to_chips(packed_tokens), packed_second + [weight], [first_rows], 0
    )
    weight = packed_second.pop()
    weights_pair = [weight, swap(weight, 1)]

    sums = project(token_pairs, weights_pair)
    received, sums = next_transfer(to_chips(packed_second), sums, (), 0)
    second_rows = place_blocks(me, to_cores(received))
    second = over_tensor(second_rows).reshape(new_split)
    terms, _ = next_transfer(to_chips(sums), [], [second_rows], 15)
    columns, columns_again = attention(lengths, terms, grad_out)

    def begin(columns):
        kept, sent = input_terms(place, columns, weights_pair)
        return kept, swap_tensor(sent, 1)

    def proceed(kept, received):
        step = 2
        while step < tensor_count:
            kept, sent = fold_terms(kept, received)
            received = swap_tensor(sent, step)
            step *= 2
        return kept, received

    near = [swap(columns, 2 * m) for m in range(1, chips - 1)]
    far = swap(gate([columns_again], near)[0] if 1 else columns, 2 * (chips - 1))
    own_state = begin([columns])
    near = gate(near, own_state[:1], 8)
    near_state = begin(near)
    if 0:
        own_state = proceed(*own_state)
    (far,) = gate([far], [own_state[0], near_state[0]], 8)
    far_state = begin([far])
    same_core = [columns, *near, far]
    all_columns = [x for pair in zip(same_core, [swap(x, 1) for x in same_core]) for x in pair]
    operands = (to_cores(token_pairs), all_columns, weight, first, second)
    some = update(*operands, 0, tensor_count // 2)
    own_state = proceed(*own_state)
    near_state = proceed(near_state[0], gate(near_state[1:], some[:1])[0])
    far_state = proceed(*far_state)
    near_sums = sum_terms(*near_state)
    new_weights, new_first, new_second = update(*operands, tensor_count // 2, tensor_count, some, near_sums[:1])
    near_sums = [swap(x, 2 * m + 2) for m, x in enumerate(near_sums)]
    (far_sum,) = sum_terms(far_state[0], gate(far_state[1:], [new_weights, *near_sums])[0])
    pairs = [*sum_terms(*own_state), *near_sums, swap(far_sum, 2 * (chips - 1))]
    input_grad = place_columns(me, [(x, at) for x in pairs for at in range(2)], (new_weights,))
    return (input_grad, new_weights, new_first, new_second)


def solution(mesh):
    return jax.shard_map(
        local,
        mesh=mesh,
        in_specs=(
            P("dp", None),
            P("dp", "tensor"),
            P("dp"),
            P("tensor", None, None, "dp"),
            P("tensor", None, None, "dp"),
            P("tensor", None, None, "dp"),
        ),
        out_specs=(
            P("dp", "tensor"),
            P(None, "dp", None, "tensor"),
            P(None, "dp", None, "tensor"),
            P(None, "dp", None, "tensor"),
        ),
        check_vma=False,
    )
```

```python
import functools

import jax
import jax.numpy as jnp
from jax import lax
from jax.experimental import pallas as pl
from jax.experimental.pallas import tpu as pltpu
from jax.sharding import PartitionSpec as P

QUERY_HEADS = 32
KEY_VALUE_HEADS = 8
HEAD_SIZE = 128


beta_first = 0.9
beta_second = 0.95
adam_eps = 1e-08
learn_rate = 0.002
decay_rate = 0.1
bias_first = 1.0 - beta_first**20
bias_second = 1.0 - beta_second**20

MIB = 1 << 20
MICROSECOND = 10**9
SMEM = pl.BlockSpec(memory_space=pltpu.SMEM)


def adam_update(param, gradient, first, second):
    first_new = beta_first * first + (1.0 - beta_first) * gradient
    second_new = beta_second * second + (1.0 - beta_second) * gradient * gradient
    ratio = first_new / bias_first / (jnp.sqrt(second_new / bias_second) + adam_eps)
    widened = param.astype(jnp.float32)
    updated = (widened - learn_rate * (ratio + decay_rate * widened)).astype(jnp.bfloat16)
    return (updated, first_new, second_new)


def shape_of(dims, dtype=jnp.bfloat16):
    return jax.ShapeDtypeStruct(dims, dtype)


def size_of(arrays):
    return sum(a.size * a.dtype.itemsize for a in arrays)


def whole_block(operand):
    if isinstance(operand, tuple):
        dims, at = operand[0].shape[1:], operand[1]
        return pl.BlockSpec((None,) + tuple(dims), lambda i: (at,) + (0,) * len(dims))
    dims = operand.shape
    return pl.BlockSpec(tuple(dims), lambda i: (0,) * len(dims))


def array_of(operand):
    return operand[0] if isinstance(operand, tuple) else operand


def whole_call(body, outs, ins, name, flops=0, scalars=1, waits=()):
    arrays = [array_of(x) for x in ins]
    moved = size_of(arrays[scalars:]) + size_of(outs)
    count = len(ins)

    def without(*refs):
        body(*refs[:count], *refs[count + len(waits) :])

    call = pl.pallas_call(
        without,
        grid=(1,),
        out_shape=outs,
        in_specs=[SMEM] * scalars
        + [whole_block(x) for x in ins[scalars:]]
        + [pl.BlockSpec(memory_space=pl.ANY)] * len(waits),
        out_specs=[whole_block(x) for x in outs],
        compiler_params=pltpu.CompilerParams(vmem_limit_bytes=60 * MIB),
        cost_estimate=pl.CostEstimate(flops=0, bytes_accessed=0, transcendentals=0),
        name=name,
    )
    return list(call(*arrays, *waits))


def pack_blocks(me, blocks, first=0, last=None):
    count, rows, columns = blocks.shape
    last = rows if last is None else last

    def body(me_ref, in_ref, *out_refs):
        for k in range(count):
            out_refs[k // 2][k % 2] = in_ref[me_ref[0] ^ k, first:last].astype(jnp.bfloat16)

    return whole_call(body, [shape_of((2, last - first, columns))] * (count // 2), [me, blocks], "pack_blocks")


def merge_rows(low, high):
    tensor_count, parts, rows, columns = low.shape

    def body(low_ref, high_ref, out_ref):
        out_ref[:, :, :rows] = low_ref[...]
        out_ref[:, :, rows:] = high_ref[...]

    outs = [shape_of((tensor_count, parts, rows + high.shape[2], columns))]
    return whole_call(body, outs, [low, high], "merge_rows", scalars=0)[0]


def gate(pieces, waits, cost=0):
    count = len(pieces)
    anywhere = pl.BlockSpec(memory_space=pl.ANY)
    return list(pl.pallas_call(
        lambda *refs: None,
        out_shape=[shape_of(x.shape, x.dtype) for x in pieces],
        in_specs=[anywhere] * (count + len(waits)),
        out_specs=[anywhere] * count,
        input_output_aliases={i: i for i in range(count)},
        cost_estimate=pl.CostEstimate(flops=cost * MICROSECOND, bytes_accessed=0, transcendentals=0),
        name="gate",
    )(*pieces, *waits))


def place_blocks(me, pieces, waits=()):
    count = len(pieces)
    dims = array_of(pieces[0]).shape[-2:]

    def body(me_ref, *refs):
        for k in range(count):
            refs[count][me_ref[0] ^ k] = refs[k][...]

    return whole_call(body, [shape_of((count,) + dims)], [me, *pieces], "place_blocks", waits=waits)[0]


def pack_columns(me, tokens, tensor_count, replica_count, waits=()):
    length, width = tokens.shape
    rows = width // (tensor_count * replica_count)
    chips = replica_count // 2
    dims = (2, length, tensor_count * rows)
    if rows % 128:
        parts = tokens.reshape(length, tensor_count, replica_count, rows).transpose(2, 0, 1, 3)
        pieces = [lax.dynamic_index_in_dim(parts, me[0] ^ k, 0, False) for k in range(replica_count)]
        return [jnp.stack(pieces[2 * m : 2 * m + 2]).reshape(dims) for m in range(chips)]

    def body(me_ref, in_ref, *out_refs):
        for k in range(replica_count):
            for t in range(tensor_count):
                start = pl.multiple_of((t * replica_count + (me_ref[0] ^ k)) * rows, rows)
                out_refs[k // 2][k % 2, :, t * rows : (t + 1) * rows] = in_ref[:, pl.ds(start, rows)]

    return whole_call(body, [shape_of(dims)] * chips, [me, tokens], "pack_columns", waits=waits)


def place_columns(me, pieces, waits=()):
    count = len(pieces)
    length, rows = array_of(pieces[0]).shape[-2:]
    if rows % 128:
        stacked = place_blocks(me, pieces)
        return stacked.transpose(1, 0, 2).reshape(length, count * rows)

    def body(me_ref, *refs):
        for k in range(count):
            start = pl.multiple_of((me_ref[0] ^ k) * rows, rows)
            refs[count][:, pl.ds(start, rows)] = refs[k][...]

    return whole_call(body, [shape_of((length, count * rows))], [me, *pieces], "place_columns", waits=waits)[0]


def swap(x, k):
    if k == 0:
        return x
    return lax.ppermute(x, "dp", [(i, i ^ k) for i in range(lax.axis_size("dp"))])


def swap_tensor(x, j):
    return lax.ppermute(x, "tensor", [(i, i ^ j) for i in range(lax.axis_size("tensor"))])


def to_chips(pairs):
    return [swap(x, 2 * m) for m, x in enumerate(pairs)]


def to_cores(pairs):
    return [view for x in pairs for view in ((x, 0), (swap(x, 1), 1))]


def over_tensor(x):
    return lax.all_to_all(x, "tensor", split_axis=0, concat_axis=0, tiled=True)


def project(pairs, weights):
    _, rows, depth = pairs[0].shape
    parts, columns = weights[0].shape[1], weights[0].shape[3]
    count = len(pairs)

    def body(*refs):
        for e in range(parts):
            blocks = [refs[count + at][:, e].reshape(depth, columns) for at in range(2)]
            for k in range(count):
                value = jnp.dot(refs[k][0], blocks[0], preferred_element_type=jnp.float32)
                value = value + jnp.dot(refs[k][1], blocks[1], preferred_element_type=jnp.float32)
                refs[count + 2 + k][:, e * columns : (e + 1) * columns] = value.astype(jnp.bfloat16)

    return whole_call(body, [shape_of((rows, parts * columns))] * count, [*pairs, *weights], "project", scalars=0)


def attention(length, terms, upstream, waits=()):
    count = len(terms)
    rows, columns = terms[0].shape
    query_columns = upstream.shape[1]
    key_value_columns = (columns - query_columns) // 2
    heads = key_value_columns // HEAD_SIZE
    group = QUERY_HEADS // KEY_VALUE_HEADS
    scale = HEAD_SIZE ** (-0.5)

    def body(length_ref, *refs):
        upstream_ref, out_refs = refs[count], refs[count + 1 :]

        def projected(start):
            cut = slice(start, start + HEAD_SIZE)
            total = refs[0][:, cut].astype(jnp.float32)
            for term in refs[1:count]:
                total = total + term[:, cut].astype(jnp.float32)
            return total.astype(jnp.bfloat16)

        def dot(a, b, on_a, on_b):
            return lax.dot_general(a, b, (((on_a,), (on_b,)), ((), ())), preferred_element_type=jnp.float32)

        def store(start, value):
            for out_ref in out_refs:
                out_ref[:, start : start + HEAD_SIZE] = value.astype(jnp.bfloat16)

        live = length_ref[0]
        at = lax.broadcasted_iota(jnp.int32, (rows, rows), 0)
        of = lax.broadcasted_iota(jnp.int32, (rows, rows), 1)
        allowed = (of <= at) & (of < live)
        active = lax.broadcasted_iota(jnp.int32, (rows, HEAD_SIZE), 0) < live
        for g in range(heads):
            key_start = query_columns + g * HEAD_SIZE
            value_start = query_columns + key_value_columns + g * HEAD_SIZE
            key, value = projected(key_start), projected(value_start)
            key_gradient = jnp.zeros((rows, HEAD_SIZE), jnp.float32)
            value_gradient = jnp.zeros((rows, HEAD_SIZE), jnp.float32)
            for n in range(group):
                start = (g * group + n) * HEAD_SIZE
                query = projected(start)
                given = upstream_ref[:, start : start + HEAD_SIZE]
                given = jnp.where(active, given, jnp.zeros_like(given))
                scores = jnp.where(allowed, dot(query, key, 1, 1) * scale, -jnp.inf)
                expo = jnp.exp(scores - jnp.max(scores, -1, keepdims=True))
                probs = expo / jnp.sum(expo, -1, keepdims=True)
                low = probs.astype(jnp.bfloat16)
                attended = dot(low, value, 1, 0)
                delta = jnp.sum(given.astype(jnp.float32) * attended, -1, keepdims=True)
                score_gradient = (probs * (dot(given, value, 1, 1) - delta) * scale).astype(jnp.bfloat16)
                store(start, dot(score_gradient, key, 1, 0))
                key_gradient = key_gradient + dot(score_gradient, query, 0, 0)
                value_gradient = value_gradient + dot(low, given, 0, 0)
            store(key_start, key_gradient)
            store(value_start, value_gradient)

    flops = 2 * heads * group * 6 * rows * rows * HEAD_SIZE
    return whole_call(body, [shape_of((rows, columns))] * 2, [length, *terms, upstream], "attention", flops, waits=waits)


def halving_order(count):
    if count == 1:
        return [0]
    half = [2 * j for j in halving_order(count // 2)]
    return half + [j + 1 for j in half]


def input_terms(place, columns, weights):
    tensor_count, parts, width, cut_columns = weights[0].shape
    count = len(columns)
    rows = columns[0].shape[0]
    half = tensor_count // 2
    order = halving_order(tensor_count)

    def body(place_ref, *refs):
        for at, j in enumerate(order):
            for core in range(2):
                blocks = [refs[count + core][place_ref[0] ^ j, e] for e in range(parts)]
                for k in range(count):
                    total = None
                    for e in range(parts):
                        term = lax.dot_general(
                            refs[k][:, e * cut_columns : (e + 1) * cut_columns],
                            blocks[e],
                            (((1,), (1,)), ((), ())),
                            preferred_element_type=jnp.float32,
                        )
                        total = term if total is None else total + term
                    refs[count + 2 + at // half][at % half, 2 * k + core] = total.astype(jnp.bfloat16)

    outs = [shape_of((half, 2 * count, rows, width))] * 2
    return whole_call(body, outs, [place, *columns, *weights], "input_terms")


def fold_terms(kept, received):
    half = kept.shape[0] // 2
    dims = (half,) + kept.shape[1:]

    def body(kept_ref, received_ref, stay_ref, go_ref):
        for at in range(2 * half):
            total = kept_ref[at].astype(jnp.float32) + received_ref[at].astype(jnp.float32)
            if at < half:
                stay_ref[at] = total
            else:
                go_ref[at - half] = total.astype(jnp.bfloat16)

    outs = [shape_of(dims, jnp.float32), shape_of(dims)]
    return whole_call(body, outs, [kept, received], "fold_terms", scalars=0)


def sum_terms(kept, received, waits=()):
    count = kept.shape[1] // 2

    def body(kept_ref, received_ref, *out_refs):
        for k in range(2 * count):
            total = kept_ref[0, k].astype(jnp.float32) + received_ref[0, k].astype(jnp.float32)
            out_refs[k // 2][k % 2] = total.astype(jnp.bfloat16)

    outs = [shape_of((2,) + kept.shape[2:])] * count
    return whole_call(body, outs, [kept, received], "sum_terms", scalars=0, waits=waits)


def update(pieces, columns, weight, first, second, begin, end, earlier=(), waits=()):
    tensor_count, parts, width, cut_columns = weight.shape
    count = len(pieces)
    rows = columns[0].shape[0]
    dims = (tensor_count, 1, width, parts * cut_columns)
    if width % 128:
        if earlier:
            return earlier
        inputs = jnp.concatenate([x[at] for x, at in pieces], 0)
        gradient = lax.dot_general(
            inputs, jnp.concatenate(columns, 0), (((0,), (0,)), ((), ())), preferred_element_type=jnp.float32
        ).reshape(dims)
        merged = [a.transpose(0, 2, 1, 3).reshape(dims) for a in (weight, first, second)]
        return adam_update(merged[0], gradient, merged[1].astype(jnp.float32), merged[2].astype(jnp.float32))

    def body(*refs):
        weight_ref, first_ref, second_ref = refs[2 * count : 2 * count + 3]
        new_weight, new_first, new_second = refs[-3:]
        gradient = None
        cut = pl.ds(pl.multiple_of(pl.program_id(1) * cut_columns, cut_columns), cut_columns)
        for k in range(count):
            term = lax.dot_general(
                refs[k][...], refs[count + k][:, cut], (((0,), (0,)), ((), ())), preferred_element_type=jnp.float32
            )
            gradient = term if gradient is None else gradient + term
        updated, moved_first, moved_second = adam_update(
            weight_ref[0, 0],
            gradient,
            first_ref[0, 0].astype(jnp.float32),
            second_ref[0, 0].astype(jnp.float32),
        )
        new_weight[0, 0] = updated
        new_first[0, 0] = moved_first
        new_second[0, 0] = moved_second

    old = pl.BlockSpec((1, 1, width, cut_columns), lambda t, e: (begin + t, e, 0, 0))
    new = pl.BlockSpec((1, 1, width, cut_columns), lambda t, e: (begin + t, 0, 0, e))
    outs = [shape_of(dims), shape_of(dims, jnp.float32), shape_of(dims, jnp.float32)]
    ins = [*map(array_of, pieces), *columns, weight, first, second, *earlier, *waits]
    given = len(ins) - len(earlier) - len(waits)
    call = pl.pallas_call(
        body,
        grid=(end - begin, parts),
        out_shape=outs,
        in_specs=[pl.BlockSpec((None, rows, width), lambda t, e, at=at: (at, 0, begin + t)) for _, at in pieces]
        + [pl.BlockSpec((rows, parts * cut_columns), lambda t, e: (0, 0))] * count
        + [old] * 3
        + [pl.BlockSpec(memory_space=pl.ANY)] * (len(earlier) + len(waits)),
        out_specs=[new] * 3,
        input_output_aliases={given + i: i for i in range(len(earlier))},
        compiler_params=pltpu.CompilerParams(vmem_limit_bytes=60 * MIB),
        cost_estimate=pl.CostEstimate(flops=0, bytes_accessed=0, transcendentals=0),
        name="update",
    )
    return list(call(*ins))


def local(tokens, grad_out, lengths, weights, moment1, moment2):
    tensor_count = lax.axis_size("tensor")
    replica_count = lax.axis_size("dp")
    width, cut_columns = weights.shape[2:]
    parts = replica_count // tensor_count
    me = lax.axis_index("dp").astype(jnp.int32).reshape(1)
    place = lax.axis_index("tensor").astype(jnp.int32).reshape(1)
    new_split = (tensor_count, parts, width, cut_columns)

    chips = replica_count // 2

    def next_transfer(received, following, meanwhile=(), cost=0):
        held = gate(received[1:] + following, meanwhile, cost)
        return received[:1] + held[: chips - 1], held[chips - 1 :]

    cut = max(width * 6 // 16 // 16, 1) * 16
    packed_low, packed_high = pack_blocks(me, weights[0], 0, cut), pack_blocks(me, weights[0], cut)
    packed_first = pack_blocks(me, moment1[0])
    packed_second = pack_blocks(me, moment2[0])
    received, packed_high = next_transfer(to_chips(packed_low), packed_high, packed_first[:1], 8)
    low_rows = place_blocks(me, to_cores(received))
    packed_tokens = pack_columns(me, tokens, tensor_count, replica_count, (low_rows,))
    received, packed_first = next_transfer(
        to_chips(packed_high), packed_first, [packed_tokens[0]], 15
    )
    high_rows = place_blocks(me, to_cores(received))
    weight = merge_rows(
        *(over_tensor(x).reshape(tensor_count, parts, x.shape[1], cut_columns) for x in (low_rows, high_rows))
    )
    received, packed_tokens = next_transfer(to_chips(packed_first), packed_tokens, [high_rows, packed_second[0]], 15)
    first_rows = place_blocks(me, to_cores(received))
    first = over_tensor(first_rows).reshape(new_split)
    token_pairs, packed_second = next_transfer(
        to_chips(packed_tokens), packed_second + [weight], [first_rows], 0
    )
    weight = packed_second.pop()
    weights_pair = [weight, swap(weight, 1)]

    sums = project(token_pairs, weights_pair)
    received, sums = next_transfer(to_chips(packed_second), sums, (), 0)
    second_rows = place_blocks(me, to_cores(received))
    second = over_tensor(second_rows).reshape(new_split)
    terms, _ = next_transfer(to_chips(sums), [], [second_rows], 15)
    columns, columns_again = attention(lengths, terms, grad_out)

    def begin(columns):
        kept, sent = input_terms(place, columns, weights_pair)
        return kept, swap_tensor(sent, 1)

    def proceed(kept, received):
        step = 2
        while step < tensor_count:
            kept, sent = fold_terms(kept, received)
            received = swap_tensor(sent, step)
            step *= 2
        return kept, received

    near = [swap(columns, 2 * m) for m in range(1, chips - 1)]
    own_state = begin([columns])
    far = swap(gate([columns_again], [*near, own_state[0]])[0], 2 * (chips - 1))
    near = gate(near, (), 8)
    near_state = begin(near)
    (far,) = gate([far], [own_state[0], near_state[0]], 8)
    far_state = begin([far])
    same_core = [columns, *near, far]
    all_columns = [x for pair in zip(same_core, [swap(x, 1) for x in same_core]) for x in pair]
    operands = (to_cores(token_pairs), all_columns, weight, first, second)
    some = update(*operands, 0, tensor_count // 2)
    own_state = proceed(*own_state)
    near_state = proceed(near_state[0], gate(near_state[1:], some[:1])[0])
    new_weights, new_first, new_second = update(*operands, tensor_count // 2, tensor_count, some, near_state[:1])
    far_state = proceed(far_state[0], gate(far_state[1:], [new_weights])[0])
    near_sums = [swap(x, 2 * m + 2) for m, x in enumerate(sum_terms(*near_state))]
    (far_sum,) = sum_terms(far_state[0], gate(far_state[1:], near_sums)[0])
    pairs = [*sum_terms(*own_state), *near_sums, swap(far_sum, 2 * (chips - 1))]
    input_grad = place_columns(me, [(x, at) for x in pairs for at in range(2)], (new_weights,))
    return (input_grad, new_weights, new_first, new_second)


def solution(mesh):
    return jax.shard_map(
        local,
        mesh=mesh,
        in_specs=(
            P("dp", None),
            P("dp", "tensor"),
            P("dp"),
            P("tensor", None, None, "dp"),
            P("tensor", None, None, "dp"),
            P("tensor", None, None, "dp"),
        ),
        out_specs=(
            P("dp", "tensor"),
            P(None, "dp", None, "tensor"),
            P(None, "dp", None, "tensor"),
            P(None, "dp", None, "tensor"),
        ),
        check_vma=False,
    )
```
